32 devices in a mesh: seq: 8 (over z, x), text: 4 (over y, core).
Axes of the slice: x: 2, y: 2, z: 4, core: 2. Of those that a mesh axis runs over, the one named last changes fastest.
Arguments:
- queries: bfloat16 [24576, 4096], P('seq', 'text'), may hold values from -2.5 to 2.5
- keys: bfloat16 [28672, 4096], P('text', 'seq'), may hold values from -2.5 to 2.5
- values: bfloat16 [28672, 4096], P('text', 'seq'), may hold values from -6 to 6
- grad_out: bfloat16 [24576, 4096], P('seq', 'text'), may hold values from -6 to 6
- res_len: int32 [64], replicated, may hold values from 1 to 384, 15360 in all
- tok_len: int32 [64], replicated, may hold values from 1 to 448, 17920 in all
Outputs:
- grad_queries: bfloat16 [24576, 4096], P('seq', 'text')
- grad_keys: bfloat16 [28672, 4096], P('text', 'seq')
- grad_values: bfloat16 [28672, 4096], P('text', 'seq')
The draws below stay inside these ranges and needn't reach their ends.
Inputs may be any that keep to these rules, and one draw needn't show every extreme that they name: Residue rows p * 384 + i with i >= res_len[p] are padding. Token rows of slot u(p) at positions j >= tok_len[p] are padding.
All inputs are finite; a program needn't handle non-finite values.
Results may differ from the reference program's by a relative error of at most 0.0054.
Values may be sent and summed in bfloat16 or wider, within the bound.
A program may use at most 128 MiB of HBM per device.

```python
import math
import jax
import jax.numpy as jnp
import numpy as np
from jax import lax

HEADS = 32
HEAD_DIM = 128
RES_SLOT = 384
TOK_SLOT = 448
PROTEINS = 64
FEAT = 4096
RES_ROWS = 24576
TOK_ROWS = 28672
N_TEXT = 4


def shard_levels(rng, dims, cuts, least, top_value):
    loudness = 1.0
    for axis_at, shards_of in cuts:
        draws = jax.random.uniform(jax.random.fold_in(jax.random.fold_in(rng, 6), axis_at), (shards_of,), jnp.float32, least / len(cuts), top_value / len(cuts))
        loudness = loudness * jnp.repeat(jnp.exp(draws), dims[axis_at] // shards_of).reshape((-1,) + (1,) * (len(dims) - 1 - axis_at))
    return loudness


def length_profile(number_of, total, reach, skew):
    weights = [(1 << 20) // math.isqrt(rank ** skew) + 1 for rank in range(2, number_of + 1)]
    rest, holding = total - reach - (number_of - 1), [1] * (number_of - 1)
    while rest > 0:
        movable = [i for i in range(number_of - 1) if holding[i] < reach]
        pool, remaining = sum([weights[i] for i in movable]), rest
        for i in movable:
            addition = min(reach - holding[i], max(1, remaining * weights[i] // pool), rest)
            holding[i] = holding[i] + addition
            rest = rest - addition
    return np.array([reach] + holding)


def uneven(own_key, count, total, reach, skew):
    if count == 2:
        one = jax.random.randint(own_key, (), max(1, total - reach), min(reach, total - 1) + 1)
        return jnp.stack([one, total - one])
    tallies = jnp.asarray(length_profile(count, total, reach, skew), jnp.int32)
    twos = (count - 1) // 2
    source_of, receiver = tallies[1:1 + 2 * twos:2], tallies[2:2 + 2 * twos:2]
    slack = jnp.minimum(source_of - 1, reach - receiver)
    shifted = jax.random.randint(jax.random.fold_in(own_key, 1), (twos,), 0, 1 << 20) % (slack + 1)
    tallies = tallies.at[1:1 + 2 * twos:2].set(source_of - shifted).at[2:2 + 2 * twos:2].set(receiver + shifted)
    return tallies[jax.random.permutation(jax.random.fold_in(own_key, 2), count)]


def gaussian(rng, extent, spread, bound, cuts=(), held_as=jnp.bfloat16):
    entries = jax.random.normal(rng, extent, jnp.float32) * spread
    if len(cuts) > 0:
        entries = shard_levels(rng, extent, cuts, -0.22, 0.18) * entries
    return jnp.clip(entries, min=-bound, max=bound).astype(held_as)


def setup_inputs(seed: int = 0) -> dict:
    key_list = jax.random.split(jax.random.key(seed), 7)
    return {
        "queries": gaussian(key_list[0], (RES_ROWS, FEAT), 1.0, 2.5, ((0, 8), (1, 4))),
        "keys": gaussian(key_list[1], (TOK_ROWS, FEAT), 1.0, 2.5, ((0, 4), (1, 8))),
        "values": gaussian(key_list[2], (TOK_ROWS, FEAT), 1.0, 6.0, ((0, 4), (1, 8))),
        "grad_out": gaussian(key_list[3], (RES_ROWS, FEAT), 1.0, 6.0, ((0, 8), (1, 4))),
        "res_len": uneven(key_list[4], PROTEINS, PROTEINS * RES_SLOT * 5 // 8, RES_SLOT, 2).astype(jnp.int32),
        "tok_len": uneven(key_list[5], PROTEINS, PROTEINS * TOK_SLOT * 5 // 8, TOK_SLOT, 2).astype(jnp.int32),
    }


def protein_backward(packed):
    q_rows, d_rows, k_rows, v_rows, rows_live, tokens_live = packed
    softmax_scale = 1.0 / math.sqrt(HEAD_DIM)
    query_heads = q_rows.astype(jnp.float32).reshape(RES_SLOT, HEADS, HEAD_DIM)
    cotangent = d_rows.astype(jnp.float32).reshape(RES_SLOT, HEADS, HEAD_DIM)
    key_heads = k_rows.astype(jnp.float32).reshape(TOK_SLOT, HEADS, HEAD_DIM)
    value_heads = v_rows.astype(jnp.float32).reshape(TOK_SLOT, HEADS, HEAD_DIM)
    scores = jnp.einsum('rhd,thd->hrt', query_heads, key_heads) * softmax_scale
    column_live = jnp.arange(TOK_SLOT, dtype=jnp.int32) < tokens_live
    row_live = jnp.arange(RES_SLOT, dtype=jnp.int32) < rows_live
    raised = jnp.where(column_live[None, None, :], jnp.exp(scores), 0.0)
    denominator = lax.optimization_barrier(jnp.sum(raised, axis=-1, keepdims=True))
    attention = jnp.where(row_live[None, :, None], raised / denominator, 0.0)
    attention_b = lax.optimization_barrier(attention.astype(jnp.bfloat16)).astype(jnp.float32)
    output = jnp.einsum('hrt,thd->rhd', attention_b, value_heads)
    delta = lax.optimization_barrier(jnp.sum(cotangent * output, axis=-1))
    grad_attention = jnp.einsum('rhd,thd->hrt', cotangent, value_heads)
    grad_scores = softmax_scale * attention * (grad_attention - delta.T[:, :, None])
    scores_b = lax.optimization_barrier(grad_scores.astype(jnp.bfloat16)).astype(jnp.float32)
    query_grads = jnp.einsum('hrt,thd->rhd', scores_b, key_heads).reshape(RES_SLOT, FEAT)
    key_grads = jnp.einsum('hrt,rhd->thd', scores_b, query_heads).reshape(TOK_SLOT, FEAT)
    value_grads = jnp.einsum('hrt,rhd->thd', attention_b, cotangent).reshape(TOK_SLOT, FEAT)
    return (query_grads.astype(jnp.bfloat16), key_grads.astype(jnp.bfloat16), value_grads.astype(jnp.bfloat16))

def to_protein_order(tokens):
    return tokens.reshape(N_TEXT, PROTEINS // N_TEXT, TOK_SLOT, FEAT).transpose(1, 0, 2, 3)

def reference(queries, keys, values, grad_out, res_len, tok_len):
    query_slots = queries.reshape(PROTEINS, RES_SLOT, FEAT)
    grad_slots = grad_out.reshape(PROTEINS, RES_SLOT, FEAT)
    key_slots = to_protein_order(keys).reshape(PROTEINS, TOK_SLOT, FEAT)
    value_slots = to_protein_order(values).reshape(PROTEINS, TOK_SLOT, FEAT)
    query_grads, key_grads, value_grads = lax.map(protein_backward, (query_slots, grad_slots, key_slots, value_slots, res_len, tok_len))
    key_grads = key_grads.reshape(PROTEINS // N_TEXT, N_TEXT, TOK_SLOT, FEAT).transpose(1, 0, 2, 3).reshape(TOK_ROWS, FEAT)
    value_grads = value_grads.reshape(PROTEINS // N_TEXT, N_TEXT, TOK_SLOT, FEAT).transpose(1, 0, 2, 3).reshape(TOK_ROWS, FEAT)
    return (query_grads.reshape(RES_ROWS, FEAT), key_grads, value_grads)
```

```python
import functools
import math

import jax
import jax.numpy as jnp
from jax import lax
from jax.experimental import pallas as pl
from jax.experimental.pallas import tpu as pltpu
from jax.sharding import PartitionSpec as P

HEAD_DIM = 128
LAG = 4


def nt(a, b):
    return lax.dot_general(a, b, (((1,), (1,)), ((), ())), preferred_element_type=jnp.float32)


def tn(a, b):
    return lax.dot_general(a, b, (((0,), (0,)), ((), ())), preferred_element_type=jnp.float32)


def kernel(
    S, T, NB, res, tok, width,
    rows_ref, toks_ref, q_ref, g_ref, k_ref, v_ref,
    dq_ref, dk_ref, dv_ref,
    far, kv, rmid, dqst, dkv,
    kv_sem, dkv_sem, fs, fr, r1s, r1r, r2s, r2r,
):
    R = S // T
    NS = S * NB
    s = lax.axis_index("seq")
    t = lax.axis_index("text")
    z = s // R
    r = s % R
    scale = 1.0 / math.sqrt(HEAD_DIM)

    for w, ref in enumerate((k_ref, v_ref)):
        pltpu.make_async_copy(ref, kv.at[w], kv_sem.at[w]).start()

    barrier = pltpu.get_barrier_semaphore()
    me = s * T + t

    def greet(d, carry):
        other = (me + d) % (S * T)
        pl.semaphore_signal(
            barrier, inc=1, device_id=(other // T, other % T),
            device_id_type=pl.DeviceIdType.MESH,
        )
        return carry

    lax.fori_loop(1, S * T, greet, 0)
    pl.semaphore_wait(barrier, S * T - 1)

    def fwd_refs(w, d, jj):
        rr = (r + d % R) % R
        tt = (t + d // R) % T
        ref = (q_ref, g_ref)[w]
        src = ref.at[jj * T + tt, :, pl.ds(pl.multiple_of(rr * width, 128), width)]
        return src, far.at[w, s * NB + jj], (t * R + rr, tt)

    def fwd_remote(w, d, jj):
        src, dst, dev = fwd_refs(w, d, jj)
        return pltpu.make_async_remote_copy(
            src_ref=src, dst_ref=dst,
            send_sem=fs.at[w, d * NB + jj], recv_sem=fr.at[w, s * NB + jj],
            device_id=dev, device_id_type=pl.DeviceIdType.MESH,
        )

    def fwd_self(d):
        return jnp.logical_and(d == 0, z == t)

    def send_fwd(m, carry):
        jj = m // (R * T)
        d = m % (R * T)
        own = fwd_self(d)

        @pl.when(own)
        def _():
            for w in range(2):
                src, dst, unused = fwd_refs(w, d, jj)
                pltpu.make_async_copy(src, dst, fr.at[w, s * NB + jj]).start()

        @pl.when(jnp.logical_not(own))
        def _():
            for w in range(2):
                fwd_remote(w, d, jj).start()

        return carry

    lax.fori_loop(0, R * T * NB, send_fwd, 0)

    def ret1(zs, rs, jj):
        return pltpu.make_async_remote_copy(
            src_ref=dqst.at[(zs * R + rs) * NB + jj],
            dst_ref=rmid.at[(z * R + rs) * NB + jj],
            send_sem=r1s.at[(zs * R + rs) * NB + jj],
            recv_sem=r1r.at[(z * R + rs) * NB + jj],
            device_id=(zs * R + r, t), device_id_type=pl.DeviceIdType.MESH,
        )

    def ret2_refs(src_buf, zf, rs, jj):
        i = (zf * R + rs) * NB + jj
        dst = dq_ref.at[jj * T + t, :, pl.ds(pl.multiple_of(r * width, 128), width)]
        return src_buf.at[i], dst, r2r.at[(jj * T + t) * R + r]

    def ret2_remote(src_buf, zf, rs, jj):
        src, dst, sem = ret2_refs(src_buf, zf, rs, jj)
        return pltpu.make_async_remote_copy(
            src_ref=src, dst_ref=dst,
            send_sem=r2s.at[(zf * R + rs) * NB + jj], recv_sem=sem,
            device_id=(z * R + rs, zf), device_id_type=pl.DeviceIdType.MESH,
        )

    def ret2_self(zf, rs):
        return jnp.logical_and(rs == r, zf == t)

    def start_ret2(src_buf, zf, rs, jj):
        own = ret2_self(zf, rs)

        @pl.when(own)
        def _():
            src, dst, sem = ret2_refs(src_buf, zf, rs, jj)
            pltpu.make_async_copy(src, dst, sem).start()

        @pl.when(jnp.logical_not(own))
        def _():
            ret2_remote(src_buf, zf, rs, jj).start()

    def order(n):
        jj = n // (T * R)
        hop = (n // R) % T
        return jj, hop, n % R

    def pass_on(n):
        jj, hop, rs = order(n)
        zf = (z + T - hop) % T

        @pl.when(hop != 0)
        def _():
            i = (zf * R + rs) * NB + jj
            pltpu.make_async_copy(rmid.at[i], rmid.at[i], r1r.at[i]).wait()
            start_ret2(rmid, zf, rs, jj)

    for w, ref in enumerate((k_ref, v_ref)):
        pltpu.make_async_copy(ref, kv.at[w], kv_sem.at[w]).wait()

    def out_copy(w, b, i):
        return pltpu.make_async_copy(
            dkv.at[w, b], (dk_ref, dv_ref)[w].at[i], dkv_sem.at[w, b]
        )

    def step(n, carry):
        jj, hop, rs = order(n)
        zs = (z + hop) % T
        i = (zs * R + rs) * NB + jj
        b = n % 2
        for w in range(2):
            pltpu.make_async_copy(far.at[w, i], far.at[w, i], fr.at[w, i]).wait()

        @pl.when(n >= 2)
        def _():
            for w in range(2):
                out_copy(w, b, i).wait()

        tok_ok = lax.broadcasted_iota(jnp.int32, (tok, 1), 0) < toks_ref[i]
        res_ok = lax.broadcasted_iota(jnp.int32, (1, res), 1) < rows_ref[i]
        for h in range(width // HEAD_DIM):
            cols = slice(h * HEAD_DIM, (h + 1) * HEAD_DIM)
            q = far[0, i, :, cols]
            g = far[1, i, :, cols]
            k = kv[0, i, :, cols]
            v = kv[1, i, :, cols]
            raised = jnp.where(tok_ok, jnp.exp(nt(k, q) * scale), 0.0)
            total = jnp.sum(raised, axis=0, keepdims=True)
            attention = raised * jnp.where(res_ok, 1.0 / total, 0.0)
            attention_b = attention.astype(jnp.bfloat16)
            grad_attention = nt(v, g)
            delta = jnp.sum(
                attention_b.astype(jnp.float32) * grad_attention, axis=0, keepdims=True
            )
            scores_b = (scale * attention * (grad_attention - delta)).astype(jnp.bfloat16)
            dkv[0, b, :, cols] = jnp.dot(
                scores_b, q, preferred_element_type=jnp.float32
            ).astype(jnp.bfloat16)
            dkv[1, b, :, cols] = jnp.dot(
                attention_b, g, preferred_element_type=jnp.float32
            ).astype(jnp.bfloat16)
            dqst[i, :, cols] = tn(k, scores_b).T.astype(jnp.bfloat16)

        @pl.when(hop == 0)
        def _():
            start_ret2(dqst, z, rs, jj)

        @pl.when(hop != 0)
        def _():
            ret1(zs, rs, jj).start()

        for w in range(2):
            out_copy(w, b, i).start()

        @pl.when(n >= LAG)
        def _():
            pass_on(n - LAG)

        return carry

    lax.fori_loop(0, NS, step, 0)

    def rest(n, carry):
        pass_on(n)
        return carry

    lax.fori_loop(NS - LAG, NS, rest, 0)

    for b in range(2):
        for w in range(2):
            out_copy(w, b, 0).wait()

    def end_fwd(m, carry):
        jj = m // (R * T)
        d = m % (R * T)

        @pl.when(jnp.logical_not(fwd_self(d)))
        def _():
            for w in range(2):
                fwd_remote(w, d, jj).wait_send()

        return carry

    lax.fori_loop(0, R * T * NB, end_fwd, 0)

    def end_ret(n, carry):
        jj, hop, rs = order(n)
        zs = (z + hop) % T

        @pl.when(hop != 0)
        def _():
            ret1(zs, rs, jj).wait_send()

        zf = (z + T - hop) % T

        @pl.when(jnp.logical_not(ret2_self(zf, rs)))
        def _():
            ret2_remote(rmid, zf, rs, jj).wait_send()

        j = n // R
        place = dq_ref.at[j, :, pl.ds(pl.multiple_of(rs * width, 128), width)]
        pltpu.make_async_copy(place, place, r2r.at[j * R + rs]).wait()
        return carry

    lax.fori_loop(0, NS, end_ret, 0)


def body(queries, keys, values, grad_out, res_len, tok_len):
    S = lax.axis_size("seq")
    T = lax.axis_size("text")
    proteins = res_len.shape[0]
    here = proteins // S
    NB = here // T
    NS = proteins // T
    res = queries.shape[0] // here
    tok = keys.shape[0] // NS
    width = keys.shape[1]
    text_block = lax.axis_index("text")

    def mine(lengths):
        return lax.dynamic_index_in_dim(lengths.reshape(NS, T), text_block, 1, keepdims=False)

    any_spec = pl.BlockSpec(memory_space=pl.ANY)
    smem = pl.BlockSpec(memory_space=pltpu.SMEM)
    dma = pltpu.SemaphoreType.DMA
    bf16 = jnp.bfloat16
    units = NS * (width // HEAD_DIM) * res * tok
    dq, dk, dv = pl.pallas_call(
        functools.partial(kernel, S, T, NB, res, tok, width),
        out_shape=(
            jax.ShapeDtypeStruct((here, res, queries.shape[1]), bf16),
            jax.ShapeDtypeStruct((NS, tok, width), bf16),
            jax.ShapeDtypeStruct((NS, tok, width), bf16),
        ),
        in_specs=[smem, smem, any_spec, any_spec, any_spec, any_spec],
        out_specs=(any_spec, any_spec, any_spec),
        scratch_shapes=[
            pltpu.VMEM((2, NS, res, width), bf16),
            pltpu.VMEM((2, NS, tok, width), bf16),
            pltpu.VMEM((NS, res, width), bf16),
            pltpu.VMEM((NS, res, width), bf16),
            pltpu.VMEM((2, 2, tok, width), bf16),
            dma((2,)),
            dma((2, 2)),
            dma((2, NS)),
            dma((2, NS)),
            dma((NS,)),
            dma((NS,)),
            dma((NS,)),
            dma((NS,)),
        ],
        compiler_params=pltpu.CompilerParams(
            collective_id=0, has_side_effects=True, vmem_limit_bytes=60 * 1024 * 1024
        ),
        cost_estimate=pl.CostEstimate(
            flops=10 * units * HEAD_DIM, bytes_accessed=8 * queries.size * 2, transcendentals=units
        ),
    )(
        mine(res_len),
        mine(tok_len),
        queries.reshape(here, res, -1),
        grad_out.reshape(here, res, -1),
        keys.reshape(NS, tok, width),
        values.reshape(NS, tok, width),
    )
    return (dq.reshape(queries.shape), dk.reshape(keys.shape), dv.reshape(values.shape))


def solution(mesh):
    return jax.shard_map(
        body,
        mesh=mesh,
        in_specs=(P("seq", "text"), P("text", "seq"), P("text", "seq"), P("seq", "text"), P(), P()),
        out_specs=(P("seq", "text"), P("text", "seq"), P("text", "seq")),
        check_vma=False,
    )
```

```python
import functools
import math

import jax
import jax.numpy as jnp
from jax import lax
from jax.experimental import pallas as pl
from jax.experimental.pallas import tpu as pltpu
from jax.sharding import PartitionSpec as P

HEAD_DIM = 128
LAG = 6


def nt(a, b):
    return lax.dot_general(a, b, (((1,), (1,)), ((), ())), preferred_element_type=jnp.float32)


def tn(a, b):
    return lax.dot_general(a, b, (((0,), (0,)), ((), ())), preferred_element_type=jnp.float32)


def kernel(
    S, T, NB, res, tok, width,
    rows_ref, toks_ref, q_ref, g_ref, k_ref, v_ref,
    dq_ref, dk_ref, dv_ref,
    far, fmid, kv, rmid, dqst, dkv,
    kv_sem, dkv_sem, fs, fr, mr, f2s, r1s, r1r, r2s, r2r,
):
    R = S // T
    NS = S * NB
    s = lax.axis_index("seq")
    t = lax.axis_index("text")
    z = s // R
    r = s % R
    scale = 1.0 / math.sqrt(HEAD_DIM)

    for w, ref in enumerate((k_ref, v_ref)):
        pltpu.make_async_copy(ref, kv.at[w], kv_sem.at[w]).start()

    barrier = pltpu.get_barrier_semaphore()
    me = s * T + t

    def greet(d, carry):
        other = (me + d) % (S * T)
        pl.semaphore_signal(
            barrier, inc=1, device_id=(other // T, other % T),
            device_id_type=pl.DeviceIdType.MESH,
        )
        return carry

    lax.fori_loop(1, S * T, greet, 0)
    pl.semaphore_wait(barrier, S * T - 1)

    def fwd_refs(w, d, jj):
        rr = (r + d % R) % R
        tt = (t + d // R) % T
        ref = (q_ref, g_ref)[w]
        src = ref.at[jj * T + tt, :, pl.ds(pl.multiple_of(rr * width, 128), width)]
        return src, rr, tt

    def fwd_copy(w, d, jj, dst, sem, plane):
        src, rr, tt = fwd_refs(w, d, jj)
        return pltpu.make_async_remote_copy(
            src_ref=src, dst_ref=dst, send_sem=fs.at[w, d * NB + jj], recv_sem=sem,
            device_id=(plane * R + rr, tt), device_id_type=pl.DeviceIdType.MESH,
        )

    def fwd_far(w, d, jj):
        i = s * NB + jj
        return fwd_copy(w, d, jj, far.at[w, i], fr.at[w, i], t)

    def fwd_near(w, d, jj):
        i = (t * R + r) * NB + jj
        return fwd_copy(w, d, jj, fmid.at[w, i], mr.at[w, i], z)

    def send_fwd(m, carry):
        jj = m // (R * T)
        d = m % (R * T)
        stays = z == t

        @pl.when(jnp.logical_and(d == 0, stays))
        def _():
            for w in range(2):
                src, rr, tt = fwd_refs(w, d, jj)
                pltpu.make_async_copy(src, far.at[w, s * NB + jj], fr.at[w, s * NB + jj]).start()

        @pl.when(jnp.logical_xor(d == 0, stays))
        def _():
            for w in range(2):
                fwd_far(w, d, jj).start()

        @pl.when(jnp.logical_and(d != 0, jnp.logical_not(stays)))
        def _():
            for w in range(2):
                fwd_near(w, d, jj).start()

        return carry

    lax.fori_loop(0, R * T * NB, send_fwd, 0)

    def order(n):
        jj = n // (T * R)
        k = (n // R) % T
        hop = ((k + T - 1) // T) * (T - 1 - k % (T - 1))
        return jj, hop, n % R

    def fwd2(w, ts, rs, jj):
        i = (ts * R + rs) * NB + jj
        o = (z * R + rs) * NB + jj
        return pltpu.make_async_remote_copy(
            src_ref=fmid.at[w, i], dst_ref=far.at[w, o],
            send_sem=f2s.at[w, i], recv_sem=fr.at[w, o],
            device_id=(ts * R + r, t), device_id_type=pl.DeviceIdType.MESH,
        )

    def passes(n):
        jj, hop, rs = order(n)
        ts = (z + T - hop) % T
        own = jnp.logical_and(rs == r, ts == t)
        return jj, rs, ts, jnp.logical_and(hop != 0, jnp.logical_not(own))

    def pass_fwd(n, carry):
        jj, rs, ts, it_does = passes(n)

        @pl.when(it_does)
        def _():
            i = (ts * R + rs) * NB + jj
            for w in range(2):
                pltpu.make_async_copy(fmid.at[w, i], fmid.at[w, i], mr.at[w, i]).wait()
                fwd2(w, ts, rs, jj).start()

        return carry

    lax.fori_loop(0, NS, pass_fwd, 0)

    def ret1(zs, rs, jj):
        return pltpu.make_async_remote_copy(
            src_ref=dqst.at[(zs * R + rs) * NB + jj],
            dst_ref=rmid.at[(z * R + rs) * NB + jj],
            send_sem=r1s.at[(zs * R + rs) * NB + jj],
            recv_sem=r1r.at[(z * R + rs) * NB + jj],
            device_id=(zs * R + r, t), device_id_type=pl.DeviceIdType.MESH,
        )

    def ret2_refs(src_buf, zf, rs, jj):
        i = (zf * R + rs) * NB + jj
        dst = dq_ref.at[jj * T + t, :, pl.ds(pl.multiple_of(r * width, 128), width)]
        return src_buf.at[i], dst, r2r.at[(jj * T + t) * R + r]

    def ret2_remote(src_buf, zf, rs, jj):
        src, dst, sem = ret2_refs(src_buf, zf, rs, jj)
        return pltpu.make_async_remote_copy(
            src_ref=src, dst_ref=dst,
            send_sem=r2s.at[(zf * R + rs) * NB + jj], recv_sem=sem,
            device_id=(z * R + rs, zf), device_id_type=pl.DeviceIdType.MESH,
        )

    def ret2_self(zf, rs):
        return jnp.logical_and(rs == r, zf == t)

    def start_ret2(src_buf, zf, rs, jj):
        own = ret2_self(zf, rs)

        @pl.when(own)
        def _():
            src, dst, sem = ret2_refs(src_buf, zf, rs, jj)
            pltpu.make_async_copy(src, dst, sem).start()

        @pl.when(jnp.logical_not(own))
        def _():
            ret2_remote(src_buf, zf, rs, jj).start()

    def pass_on(n):
        jj, hop, rs = order(n)
        zf = (z + T - hop) % T

        @pl.when(hop != 0)
        def _():
            i = (zf * R + rs) * NB + jj
            pltpu.make_async_copy(rmid.at[i], rmid.at[i], r1r.at[i]).wait()
            start_ret2(rmid, zf, rs, jj)

    for w, ref in enumerate((k_ref, v_ref)):
        pltpu.make_async_copy(ref, kv.at[w], kv_sem.at[w]).wait()

    def out_copy(w, b, i):
        return pltpu.make_async_copy(
            dkv.at[w, b], (dk_ref, dv_ref)[w].at[i], dkv_sem.at[w, b]
        )

    def step(n, carry):
        jj, hop, rs = order(n)
        zs = (z + hop) % T
        i = (zs * R + rs) * NB + jj
        b = n % 2
        for w in range(2):
            pltpu.make_async_copy(far.at[w, i], far.at[w, i], fr.at[w, i]).wait()

        @pl.when(n >= 2)
        def _():
            for w in range(2):
                out_copy(w, b, i).wait()

        tok_ok = lax.broadcasted_iota(jnp.int32, (tok, 1), 0) < toks_ref[i]
        res_ok = lax.broadcasted_iota(jnp.int32, (1, res), 1) < rows_ref[i]
        for h in range(width // HEAD_DIM):
            cols = slice(h * HEAD_DIM, (h + 1) * HEAD_DIM)
            q = far[0, i, :, cols]
            g = far[1, i, :, cols]
            k = kv[0, i, :, cols]
            v = kv[1, i, :, cols]
            raised = jnp.where(tok_ok, jnp.exp(nt(k, q) * scale), 0.0)
            total = jnp.sum(raised, axis=0, keepdims=True)
            attention = raised * jnp.where(res_ok, 1.0 / total, 0.0)
            attention_b = attention.astype(jnp.bfloat16)
            grad_attention = nt(v, g)
            delta = jnp.sum(
                attention_b.astype(jnp.float32) * grad_attention, axis=0, keepdims=True
            )
            scores_b = (scale * attention * (grad_attention - delta)).astype(jnp.bfloat16)
            dkv[0, b, :, cols] = jnp.dot(
                scores_b, q, preferred_element_type=jnp.float32
            ).astype(jnp.bfloat16)
            dkv[1, b, :, cols] = jnp.dot(
                attention_b, g, preferred_element_type=jnp.float32
            ).astype(jnp.bfloat16)
            dqst[i, :, cols] = tn(k, scores_b).T.astype(jnp.bfloat16)

        @pl.when(hop == 0)
        def _():
            start_ret2(dqst, z, rs, jj)

        @pl.when(hop != 0)
        def _():
            ret1(zs, rs, jj).start()

        for w in range(2):
            out_copy(w, b, i).start()

        @pl.when(n >= LAG)
        def _():
            pass_on(n - LAG)

        return carry

    lax.fori_loop(0, NS, step, 0)

    def rest(n, carry):
        pass_on(n)
        return carry

    lax.fori_loop(NS - LAG, NS, rest, 0)

    for b in range(2):
        for w in range(2):
            out_copy(w, b, 0).wait()

    def end_fwd(m, carry):
        jj = m // (R * T)
        d = m % (R * T)

        @pl.when(jnp.logical_not(jnp.logical_and(d == 0, z == t)))
        def _():
            for w in range(2):
                fwd_far(w, d, jj).wait_send()

        return carry

    lax.fori_loop(0, R * T * NB, end_fwd, 0)

    def end_pass(n, carry):
        jj, rs, ts, it_does = passes(n)

        @pl.when(it_does)
        def _():
            for w in range(2):
                fwd2(w, ts, rs, jj).wait_send()

        return carry

    lax.fori_loop(0, NS, end_pass, 0)

    def end_ret(n, carry):
        jj, hop, rs = order(n)
        zs = (z + hop) % T

        @pl.when(hop != 0)
        def _():
            ret1(zs, rs, jj).wait_send()

        zf = (z + T - hop) % T

        @pl.when(jnp.logical_not(ret2_self(zf, rs)))
        def _():
            ret2_remote(rmid, zf, rs, jj).wait_send()

        j = n // R
        place = dq_ref.at[j, :, pl.ds(pl.multiple_of(rs * width, 128), width)]
        pltpu.make_async_copy(place, place, r2r.at[j * R + rs]).wait()
        return carry

    lax.fori_loop(0, NS, end_ret, 0)


def body(queries, keys, values, grad_out, res_len, tok_len):
    S = lax.axis_size("seq")
    T = lax.axis_size("text")
    proteins = res_len.shape[0]
    here = proteins // S
    NB = here // T
    NS = proteins // T
    res = queries.shape[0] // here
    tok = keys.shape[0] // NS
    width = keys.shape[1]
    text_block = lax.axis_index("text")

    def mine(lengths):
        return lax.dynamic_index_in_dim(lengths.reshape(NS, T), text_block, 1, keepdims=False)

    any_spec = pl.BlockSpec(memory_space=pl.ANY)
    smem = pl.BlockSpec(memory_space=pltpu.SMEM)
    dma = pltpu.SemaphoreType.DMA
    bf16 = jnp.bfloat16
    units = NS * (width // HEAD_DIM) * res * tok
    dq, dk, dv = pl.pallas_call(
        functools.partial(kernel, S, T, NB, res, tok, width),
        out_shape=(
            jax.ShapeDtypeStruct((here, res, queries.shape[1]), bf16),
            jax.ShapeDtypeStruct((NS, tok, width), bf16),
            jax.ShapeDtypeStruct((NS, tok, width), bf16),
        ),
        in_specs=[smem, smem, any_spec, any_spec, any_spec, any_spec],
        out_specs=(any_spec, any_spec, any_spec),
        scratch_shapes=[
            pltpu.VMEM((2, NS, res, width), bf16),
            pltpu.VMEM((2, NS, res, width), bf16),
            pltpu.VMEM((2, NS, tok, width), bf16),
            pltpu.VMEM((NS, res, width), bf16),
            pltpu.VMEM((NS, res, width), bf16),
            pltpu.VMEM((2, 2, tok, width), bf16),
            dma((2,)),
            dma((2, 2)),
            dma((2, NS)),
            dma((2, NS)),
            dma((2, NS)),
            dma((2, NS)),
            dma((NS,)),
            dma((NS,)),
            dma((NS,)),
            dma((NS,)),
        ],
        compiler_params=pltpu.CompilerParams(
            collective_id=0, has_side_effects=True, vmem_limit_bytes=60 * 1024 * 1024
        ),
        cost_estimate=pl.CostEstimate(
            flops=10 * units * HEAD_DIM, bytes_accessed=8 * queries.size * 2, transcendentals=units
        ),
    )(
        mine(res_len),
        mine(tok_len),
        queries.reshape(here, res, -1),
        grad_out.reshape(here, res, -1),
        keys.reshape(NS, tok, width),
        values.reshape(NS, tok, width),
    )
    return (dq.reshape(queries.shape), dk.reshape(keys.shape), dv.reshape(values.shape))


def solution(mesh):
    return jax.shard_map(
        body,
        mesh=mesh,
        in_specs=(P("seq", "text"), P("text", "seq"), P("text", "seq"), P("seq", "text"), P(), P()),
        out_specs=(P("seq", "text"), P("text", "seq"), P("text", "seq")),
        check_vma=False,
    )
```

```python
import functools
import math

import jax
import jax.numpy as jnp
from jax import lax
from jax.experimental import pallas as pl
from jax.experimental.pallas import tpu as pltpu
from jax.sharding import PartitionSpec as P

HEAD_DIM = 128
LAG = 6


def nt(a, b):
    return lax.dot_general(a, b, (((1,), (1,)), ((), ())), preferred_element_type=jnp.float32)


def tn(a, b):
    return lax.dot_general(a, b, (((0,), (0,)), ((), ())), preferred_element_type=jnp.float32)


def kernel(
    S, T, NB, res, tok, width,
    rows_ref, toks_ref, q_ref, g_ref, k_ref, v_ref,
    dq_ref, dk_ref, dv_ref,
    far, fmid, kv, rmid, dqst, dkv,
    kv_sem, dkv_sem, fs, fr, mr, f2s, r1s, r1r, r2s, r2r,
):
    R = S // T
    NS = S * NB
    s = lax.axis_index("seq")
    t = lax.axis_index("text")
    z = s // R
    r = s % R
    scale = 1.0 / math.sqrt(HEAD_DIM)

    for w, ref in enumerate((k_ref, v_ref)):
        pltpu.make_async_copy(ref, kv.at[w], kv_sem.at[w]).start()

    barrier = pltpu.get_barrier_semaphore()
    me = s * T + t

    def greet(d, carry):
        other = (me + d) % (S * T)
        pl.semaphore_signal(
            barrier, inc=1, device_id=(other // T, other % T),
            device_id_type=pl.DeviceIdType.MESH,
        )
        return carry

    lax.fori_loop(1, S * T, greet, 0)
    pl.semaphore_wait(barrier, S * T - 1)

    def fwd_refs(w, d, jj):
        rr = (r + d % R) % R
        tt = (t + d // R) % T
        ref = (q_ref, g_ref)[w]
        src = ref.at[jj * T + tt, :, pl.ds(pl.multiple_of(rr * width, 128), width)]
        return src, rr, tt

    def fwd_copy(w, d, jj, dst, sem, plane):
        src, rr, tt = fwd_refs(w, d, jj)
        return pltpu.make_async_remote_copy(
            src_ref=src, dst_ref=dst, send_sem=fs.at[w, d * NB + jj], recv_sem=sem,
            device_id=(plane * R + rr, tt), device_id_type=pl.DeviceIdType.MESH,
        )

    def fwd_far(w, d, jj):
        i = s * NB + jj
        return fwd_copy(w, d, jj, far.at[w, i], fr.at[w, i], t)

    def fwd_near(w, d, jj):
        i = (t * R + r) * NB + jj
        return fwd_copy(w, d, jj, fmid.at[w, i], mr.at[w, i], z)

    def turn(a):
        return (a % 2) * (T // 2) + a // 2 if T % 2 == 0 else a

    def send_fwd(m, carry):
        jj = m // (R * T)
        d = turn(m // R % T) * R + m % R
        stays = z == t

        @pl.when(jnp.logical_and(d == 0, stays))
        def _():
            for w in range(2):
                src, rr, tt = fwd_refs(w, d, jj)
                pltpu.make_async_copy(src, far.at[w, s * NB + jj], fr.at[w, s * NB + jj]).start()

        @pl.when(jnp.logical_xor(d == 0, stays))
        def _():
            for w in range(2):
                fwd_far(w, d, jj).start()

        @pl.when(jnp.logical_and(d != 0, jnp.logical_not(stays)))
        def _():
            for w in range(2):
                fwd_near(w, d, jj).start()

        return carry

    lax.fori_loop(0, R * T * NB, send_fwd, 0)

    def order(n):
        jj = n // (T * R)
        k = (n // R) % T
        hop = ((k + T - 1) // T) * (T - 1 - k % (T - 1))
        return jj, hop, n % R

    def fwd2(w, ts, rs, jj):
        i = (ts * R + rs) * NB + jj
        o = (z * R + rs) * NB + jj
        return pltpu.make_async_remote_copy(
            src_ref=fmid.at[w, i], dst_ref=far.at[w, o],
            send_sem=f2s.at[w, i], recv_sem=fr.at[w, o],
            device_id=(ts * R + r, t), device_id_type=pl.DeviceIdType.MESH,
        )

    def passes(n):
        jj = n // (T * R)
        rs = n % R
        ts = (t + T - turn(n // R % T)) % T
        own = jnp.logical_and(rs == r, ts == t)
        return jj, rs, ts, jnp.logical_and(ts != z, jnp.logical_not(own))

    def pass_fwd(n, carry):
        jj, rs, ts, it_does = passes(n)

        @pl.when(it_does)
        def _():
            i = (ts * R + rs) * NB + jj
            for w in range(2):
                pltpu.make_async_copy(fmid.at[w, i], fmid.at[w, i], mr.at[w, i]).wait()
                fwd2(w, ts, rs, jj).start()

        return carry

    lax.fori_loop(0, NS, pass_fwd, 0)

    def ret1(zs, rs, jj):
        return pltpu.make_async_remote_copy(
            src_ref=dqst.at[(zs * R + rs) * NB + jj],
            dst_ref=rmid.at[(z * R + rs) * NB + jj],
            send_sem=r1s.at[(zs * R + rs) * NB + jj],
            recv_sem=r1r.at[(z * R + rs) * NB + jj],
            device_id=(zs * R + r, t), device_id_type=pl.DeviceIdType.MESH,
        )

    def ret2_refs(src_buf, zf, rs, jj):
        i = (zf * R + rs) * NB + jj
        dst = dq_ref.at[jj * T + t, :, pl.ds(pl.multiple_of(r * width, 128), width)]
        return src_buf.at[i], dst, r2r.at[(jj * T + t) * R + r]

    def ret2_remote(src_buf, zf, rs, jj):
        src, dst, sem = ret2_refs(src_buf, zf, rs, jj)
        return pltpu.make_async_remote_copy(
            src_ref=src, dst_ref=dst,
            send_sem=r2s.at[(zf * R + rs) * NB + jj], recv_sem=sem,
            device_id=(z * R + rs, zf), device_id_type=pl.DeviceIdType.MESH,
        )

    def ret2_self(zf, rs):
        return jnp.logical_and(rs == r, zf == t)

    def start_ret2(src_buf, zf, rs, jj):
        own = ret2_self(zf, rs)

        @pl.when(own)
        def _():
            src, dst, sem = ret2_refs(src_buf, zf, rs, jj)
            pltpu.make_async_copy(src, dst, sem).start()

        @pl.when(jnp.logical_not(own))
        def _():
            ret2_remote(src_buf, zf, rs, jj).start()

    def pass_on(n):
        jj, hop, rs = order(n)
        zf = (z + T - hop) % T

        @pl.when(hop != 0)
        def _():
            i = (zf * R + rs) * NB + jj
            pltpu.make_async_copy(rmid.at[i], rmid.at[i], r1r.at[i]).wait()
            start_ret2(rmid, zf, rs, jj)

    for w, ref in enumerate((k_ref, v_ref)):
        pltpu.make_async_copy(ref, kv.at[w], kv_sem.at[w]).wait()

    def out_copy(w, b, i):
        return pltpu.make_async_copy(
            dkv.at[w, b], (dk_ref, dv_ref)[w].at[i], dkv_sem.at[w, b]
        )

    def step(n, carry):
        jj, hop, rs = order(n)
        zs = (z + hop) % T
        i = (zs * R + rs) * NB + jj
        b = n % 2
        for w in range(2):
            pltpu.make_async_copy(far.at[w, i], far.at[w, i], fr.at[w, i]).wait()

        @pl.when(n >= 2)
        def _():
            for w in range(2):
                out_copy(w, b, i).wait()

        tok_ok = lax.broadcasted_iota(jnp.int32, (tok, 1), 0) < toks_ref[i]
        res_ok = lax.broadcasted_iota(jnp.int32, (1, res), 1) < rows_ref[i]
        for h in range(width // HEAD_DIM):
            cols = slice(h * HEAD_DIM, (h + 1) * HEAD_DIM)
            q = far[0, i, :, cols]
            g = far[1, i, :, cols]
            k = kv[0, i, :, cols]
            v = kv[1, i, :, cols]
            raised = jnp.where(tok_ok, jnp.exp(nt(k, q) * scale), 0.0)
            total = jnp.sum(raised, axis=0, keepdims=True)
            attention = raised * jnp.where(res_ok, 1.0 / total, 0.0)
            attention_b = attention.astype(jnp.bfloat16)
            grad_attention = nt(v, g)
            delta = jnp.sum(
                attention_b.astype(jnp.float32) * grad_attention, axis=0, keepdims=True
            )
            scores_b = (scale * attention * (grad_attention - delta)).astype(jnp.bfloat16)
            dkv[0, b, :, cols] = jnp.dot(
                scores_b, q, preferred_element_type=jnp.float32
            ).astype(jnp.bfloat16)
            dkv[1, b, :, cols] = jnp.dot(
                attention_b, g, preferred_element_type=jnp.float32
            ).astype(jnp.bfloat16)
            dqst[i, :, cols] = tn(k, scores_b).T.astype(jnp.bfloat16)

        @pl.when(hop == 0)
        def _():
            start_ret2(dqst, z, rs, jj)

        @pl.when(hop != 0)
        def _():
            ret1(zs, rs, jj).start()

        for w in range(2):
            out_copy(w, b, i).start()

        @pl.when(n >= LAG)
        def _():
            pass_on(n - LAG)

        return carry

    lax.fori_loop(0, NS, step, 0)

    def rest(n, carry):
        pass_on(n)
        return carry

    lax.fori_loop(NS - LAG, NS, rest, 0)

    for b in range(2):
        for w in range(2):
            out_copy(w, b, 0).wait()

    def end_fwd(m, carry):
        jj = m // (R * T)
        d = m % (R * T)

        @pl.when(jnp.logical_not(jnp.logical_and(d == 0, z == t)))
        def _():
            for w in range(2):
                fwd_far(w, d, jj).wait_send()

        return carry

    lax.fori_loop(0, R * T * NB, end_fwd, 0)

    def end_pass(n, carry):
        jj, rs, ts, it_does = passes(n)

        @pl.when(it_does)
        def _():
            for w in range(2):
                fwd2(w, ts, rs, jj).wait_send()

        return carry

    lax.fori_loop(0, NS, end_pass, 0)

    def end_ret(n, carry):
        jj, hop, rs = order(n)
        zs = (z + hop) % T

        @pl.when(hop != 0)
        def _():
            ret1(zs, rs, jj).wait_send()

        zf = (z + T - hop) % T

        @pl.when(jnp.logical_not(ret2_self(zf, rs)))
        def _():
            ret2_remote(rmid, zf, rs, jj).wait_send()

        j = n // R
        place = dq_ref.at[j, :, pl.ds(pl.multiple_of(rs * width, 128), width)]
        pltpu.make_async_copy(place, place, r2r.at[j * R + rs]).wait()
        return carry

    lax.fori_loop(0, NS, end_ret, 0)


def body(queries, keys, values, grad_out, res_len, tok_len):
    S = lax.axis_size("seq")
    T = lax.axis_size("text")
    proteins = res_len.shape[0]
    here = proteins // S
    NB = here // T
    NS = proteins // T
    res = queries.shape[0] // here
    tok = keys.shape[0] // NS
    width = keys.shape[1]
    text_block = lax.axis_index("text")

    def mine(lengths):
        return lax.dynamic_index_in_dim(lengths.reshape(NS, T), text_block, 1, keepdims=False)

    any_spec = pl.BlockSpec(memory_space=pl.ANY)
    smem = pl.BlockSpec(memory_space=pltpu.SMEM)
    dma = pltpu.SemaphoreType.DMA
    bf16 = jnp.bfloat16
    units = NS * (width // HEAD_DIM) * res * tok
    dq, dk, dv = pl.pallas_call(
        functools.partial(kernel, S, T, NB, res, tok, width),
        out_shape=(
            jax.ShapeDtypeStruct((here, res, queries.shape[1]), bf16),
            jax.ShapeDtypeStruct((NS, tok, width), bf16),
            jax.ShapeDtypeStruct((NS, tok, width), bf16),
        ),
        in_specs=[smem, smem, any_spec, any_spec, any_spec, any_spec],
        out_specs=(any_spec, any_spec, any_spec),
        scratch_shapes=[
            pltpu.VMEM((2, NS, res, width), bf16),
            pltpu.VMEM((2, NS, res, width), bf16),
            pltpu.VMEM((2, NS, tok, width), bf16),
            pltpu.VMEM((NS, res, width), bf16),
            pltpu.VMEM((NS, res, width), bf16),
            pltpu.VMEM((2, 2, tok, width), bf16),
            dma((2,)),
            dma((2, 2)),
            dma((2, NS)),
            dma((2, NS)),
            dma((2, NS)),
            dma((2, NS)),
            dma((NS,)),
            dma((NS,)),
            dma((NS,)),
            dma((NS,)),
        ],
        compiler_params=pltpu.CompilerParams(
            collective_id=0, has_side_effects=True, vmem_limit_bytes=60 * 1024 * 1024
        ),
        cost_estimate=pl.CostEstimate(
            flops=10 * units * HEAD_DIM, bytes_accessed=8 * queries.size * 2, transcendentals=units
        ),
    )(
        mine(res_len),
        mine(tok_len),
        queries.reshape(here, res, -1),
        grad_out.reshape(here, res, -1),
        keys.reshape(NS, tok, width),
        values.reshape(NS, tok, width),
    )
    return (dq.reshape(queries.shape), dk.reshape(keys.shape), dv.reshape(values.shape))


def solution(mesh):
    return jax.shard_map(
        body,
        mesh=mesh,
        in_specs=(P("seq", "text"), P("text", "seq"), P("text", "seq"), P("seq", "text"), P(), P()),
        out_specs=(P("seq", "text"), P("text", "seq"), P("text", "seq")),
        check_vma=False,
    )
```
